512 devices in a mesh: blk: 128 (over x_hi, z, y), chan: 4 (over x_lo, core).
Axes of the slice: x: 4 (x_hi: 2, x_lo: 2; x = x_hi * 2 + x_lo), y: 8, z: 8, core: 2. Of those that a mesh axis runs over, the one named last changes fastest.
Arguments:
- student: bfloat16 [16384, 256], P('blk', 'chan'), may hold values from -11 to 11
- teacher: bfloat16 [16384, 256], P('blk', 'chan'), may hold values from -11 to 11
Outputs:
- student_grad: float32 [16384, 256], P('blk', 'chan')
The draws below stay inside these ranges and needn't reach their ends.
All inputs are finite; a program needn't handle non-finite values.
Results may differ from the reference program's by a relative error of at most 0.002.
Values may be sent and summed in bfloat16 or wider, within the bound.
No kernel may reach another device: no remote copies, remote signals or barrier semaphores. Data moves between devices by JAX's collectives and lax.ppermute only.
A program may use at most 64 MiB of HBM per device.

```python
import math
import jax
import jax.numpy as jnp
from jax import lax

C = 256
N = 16384


def draw_student(key, part):
    key = jax.random.fold_in(key, 11)
    first = jax.random.fold_in(key, 0)
    base = jax.random.truncated_normal(first, -4.0, 4.0, (N, C), jnp.float32)
    return base.astype(jnp.bfloat16)


def draw_teacher(key, part):
    key = jax.random.fold_in(key, 23)
    first = jax.random.fold_in(key, 0)
    base = jax.random.truncated_normal(first, -4.0, 4.0, (N, C), jnp.float32)
    return base.astype(jnp.bfloat16)


def setup_inputs(seed: int = 0) -> dict:
    streams_of = jax.random.split(jax.random.key(seed), 3)
    student = draw_student(jax.random.fold_in(streams_of[2], 71), 0)
    teacher = draw_teacher(jax.random.fold_in(streams_of[2], 71), 0)
    return dict(student=student, teacher=teacher)


inverse_temp = 0.125


def reference(student, teacher):
    total = student.shape[0]
    block = math.gcd(total, 512)
    count = total // block
    key_index = jnp.arange(total, dtype=jnp.int32)

    def softmax_rows(score):
        top = jnp.max(score, axis=1, keepdims=True)
        expo = jnp.exp(score - top)
        return expo / jnp.sum(expo, axis=1, keepdims=True)

    def one_block(col_acc, index):
        start = (index * block).astype(jnp.int32)
        stud_rows = lax.dynamic_slice_in_dim(student, start, block, 0)
        teach_rows = lax.dynamic_slice_in_dim(teacher, start, block, 0)
        query_index = start + jnp.arange(block, dtype=jnp.int32)
        self_pair = query_index[:, None] == key_index[None, :]
        stud_score = jnp.dot(stud_rows, student.T, preferred_element_type=jnp.float32) * inverse_temp
        teach_score = jnp.dot(teach_rows, teacher.T, preferred_element_type=jnp.float32) * inverse_temp
        stud_score = jnp.where(self_pair, -1e30, stud_score)
        teach_score = jnp.where(self_pair, -1e30, teach_score)
        grad_tile = (softmax_rows(stud_score) - softmax_rows(teach_score)).astype(jnp.bfloat16)
        row_term = jnp.dot(grad_tile, student, preferred_element_type=jnp.float32)
        col_acc = col_acc + jnp.dot(grad_tile.T, stud_rows, preferred_element_type=jnp.float32)
        return col_acc, row_term

    col_term, row_blocks = lax.scan(one_block, jnp.zeros(student.shape, jnp.float32), jnp.arange(count, dtype=jnp.int32))
    row_term = row_blocks.reshape(student.shape)
    return inverse_temp * (row_term + col_term)
```

```python
import jax
import jax.numpy as jnp
from jax import lax
from jax.experimental import pallas as pl
from jax.experimental.pallas import tpu as pltpu
from jax.sharding import Mesh, PartitionSpec as P

inverse_temp = 0.125
ROW_BLOCKS = 8
KEYS = 512
QUARTER = 32
CHAN = ("xl", "core")
f32, bf16 = jnp.float32, jnp.bfloat16


def fill_scores(place, rows_ref, keys_ref, score):
    for t in range(2):
        keys = keys_ref[:, t * 256 : (t + 1) * 256]
        for b in range(ROW_BLOCKS):
            rows = jnp.concatenate([rows_ref[b, c, t] for c in range(4)], axis=0)
            score[t, b] = jnp.dot(keys, rows, preferred_element_type=f32) * inverse_temp
    block = place[0]
    first = pl.multiple_of(place[1], QUARTER)
    lane = lax.broadcasted_iota(jnp.int32, (QUARTER, 128), 1) - place[2]
    same = lane == lax.broadcasted_iota(jnp.int32, (QUARTER, 128), 0)
    for t in range(2):
        old = score[t, block, pl.ds(first, QUARTER), :]
        score[t, block, pl.ds(first, QUARTER), :] = jnp.where(same, -1e30, old)


def stats_kernel(place, rows_ref, keys_ref, row_out, col_out, score):
    fill_scores(place, rows_ref, keys_ref, score)
    row_parts, col_parts = [], []
    for t in range(2):
        top = score[t, 0]
        for b in range(1, ROW_BLOCKS):
            top = jnp.maximum(top, score[t, b])
        col_sum = jnp.zeros((KEYS, 128), f32)
        for b in range(ROW_BLOCKS):
            s = score[t, b]
            row_max = jnp.max(s, axis=0, keepdims=True)
            row_sum = jnp.sum(jnp.exp(s - row_max), axis=0, keepdims=True)
            row_parts.append(row_max + jnp.log(row_sum))
            col_sum = col_sum + jnp.exp(s - top)
        top_t, sum_t = top.T, col_sum.T
        col_max = jnp.max(top_t, axis=0, keepdims=True)
        col_tot = jnp.sum(sum_t * jnp.exp(top_t - col_max), axis=0, keepdims=True)
        col = col_max + jnp.log(col_tot)
        col_parts += [col[:, q * 128 : (q + 1) * 128] for q in range(4)]
    row = jnp.concatenate(row_parts, axis=0)
    col = jnp.concatenate(col_parts, axis=0)
    row_out[...] = jnp.broadcast_to(row[None], row_out.shape)
    col_out[...] = jnp.broadcast_to(col[None], col_out.shape)


def combine(parts):
    top = jnp.max(parts, axis=0)
    return top + jnp.log(jnp.sum(jnp.exp(parts - top[None]), axis=0))


def grad_kernel(place, rows_ref, keys_ref, row_in, col_in, out, score):
    fill_scores(place, rows_ref, keys_ref, score)
    row = combine(row_in[...])
    col = combine(col_in[...])

    def key_column(t):
        return jnp.concatenate(
            [jnp.broadcast_to(col[t * 4 + q : t * 4 + q + 1], (128, 128)).T for q in range(4)], axis=0
        )

    cols = [key_column(t) for t in range(2)]
    keys_t = keys_ref[:, 0:256].T
    for b in range(ROW_BLOCKS):
        prob = []
        for t in range(2):
            s = score[t, b]
            prob.append(jnp.exp(s - row[t * 8 + b : t * 8 + b + 1]) + jnp.exp(s - cols[t]))
        tile = prob[0] - prob[1]
        high = tile.astype(bf16)
        low = (tile - high.astype(f32)).astype(bf16)
        part = jnp.dot(keys_t, high, preferred_element_type=f32)
        part = part + jnp.dot(keys_t, low, preferred_element_type=f32)
        out[b] = part.astype(bf16)


VMEM = pl.BlockSpec(memory_space=pltpu.VMEM)
SMEM = pl.BlockSpec(memory_space=pltpu.SMEM)
SCORE = pltpu.VMEM((2, ROW_BLOCKS, KEYS, 128), f32)
PARAMS = pltpu.CompilerParams(vmem_limit_bytes=40 * 1024 * 1024)


def body(student, teacher):
    xh, z, y = lax.axis_index("xh"), lax.axis_index("z"), lax.axis_index("y")
    chan = lax.axis_index(CHAN)
    place = jnp.stack([y, (xh * 8 + z) * QUARTER, chan * QUARTER]).astype(jnp.int32)
    mine = jnp.concatenate([student.T, teacher.T], axis=0)
    own = lax.all_gather(mine, CHAN, axis=0, tiled=True)
    flipped = own.reshape(4, 2, 64, 128).transpose(3, 1, 0, 2).reshape(128, 512)
    share = lax.dynamic_slice_in_dim(flipped, chan * QUARTER, QUARTER, 0)
    keys = lax.all_to_all(
        jnp.broadcast_to(share[None], (16, QUARTER, 512)), ("xh", "z"), split_axis=0, concat_axis=0
    ).reshape(KEYS, 512)
    rows = lax.all_gather(own, "y", axis=0, tiled=True).reshape(8, 4, 2, 64, 128)
    row_part, col_part = pl.pallas_call(
        stats_kernel,
        out_shape=(
            jax.ShapeDtypeStruct((32, 16, 128), f32),
            jax.ShapeDtypeStruct((16, 8, 128), f32),
        ),
        in_specs=[SMEM, VMEM, VMEM],
        out_specs=(VMEM, VMEM),
        scratch_shapes=[SCORE],
        compiler_params=PARAMS,
    )(place, rows, keys)
    row_all = lax.all_to_all(row_part, ("y", "xl", "core"), split_axis=0, concat_axis=0)
    col_all = lax.all_to_all(col_part, ("xh", "z"), split_axis=0, concat_axis=0)
    part = pl.pallas_call(
        grad_kernel,
        out_shape=jax.ShapeDtypeStruct((ROW_BLOCKS, 256, 128), bf16),
        in_specs=[SMEM, VMEM, VMEM, VMEM, VMEM],
        out_specs=VMEM,
        scratch_shapes=[SCORE],
        compiler_params=PARAMS,
    )(place, rows, keys, row_all, col_all)
    got = lax.all_to_all(
        part.reshape(32, 64, 128), ("y", "xl", "core"), split_axis=0, concat_axis=0
    )
    return (inverse_temp * jnp.sum(got.astype(f32), axis=0)).T


def solution(mesh):
    split = Mesh(mesh.devices.reshape(2, 8, 8, 2, 2), ("xh", "z", "y", "xl", "core"))
    spec = P(("xh", "z", "y"), CHAN)
    return jax.shard_map(
        body, mesh=split, in_specs=(spec, spec), out_specs=spec, check_vma=False
    )
```

```python
import jax
import jax.numpy as jnp
from jax import lax
from jax.experimental import pallas as pl
from jax.experimental.pallas import tpu as pltpu
from jax.sharding import Mesh, PartitionSpec as P

inverse_temp = 0.125
AXES = ("xh", "z", "y", "xl", "core")
SIZES = (2, 8, 8, 2, 2)
CHAN = ("xl", "core")
HALF = 64
ROWS = 512
KEYS = 1024
WIDE = 256
BLOCKS = KEYS // WIDE
f32, bf16 = jnp.float32, jnp.bfloat16


def device(xh, z, y, xl, core):
    return (((xh * 8 + z) * 8 + y) * 2 + xl) * 2 + core


MIXED = [
    [device(xh, z, y, xl, 0) for y in range(8) for xl in range(2)] for xh in range(2) for z in range(8)
] + [[device(xh, z, y, xl, 1) for xh in range(2) for z in range(8)] for y in range(8) for xl in range(2)]


def mixed_exchange(pieces):
    return lax.all_to_all(pieces, AXES, split_axis=0, concat_axis=0, axis_index_groups=MIXED)


def fill_scores(place, data, score):
    core = place[0]
    for t in range(2):
        cut = slice(t * 256, (t + 1) * 256)
        rows = jnp.concatenate([data[0, 2 * y + core, :, cut] for y in range(8)], axis=0)
        for b in range(BLOCKS):
            keys = jnp.concatenate([data[1, 4 * b + k, :, cut] for k in range(4)], axis=0)
            score[t, b] = (
                lax.dot_general(rows, keys, (((1,), (1,)), ((), ())), preferred_element_type=f32)
                * inverse_temp
            )
    first = pl.multiple_of(place[1], HALF)
    lane = lax.broadcasted_iota(jnp.int32, (HALF, WIDE), 1) - place[3]
    same = lane == lax.broadcasted_iota(jnp.int32, (HALF, WIDE), 0)
    for t in range(2):
        old = score[t, place[2], pl.ds(first, HALF), :]
        score[t, place[2], pl.ds(first, HALF), :] = jnp.where(same, -1e30, old)


def stats_kernel(place, data, out, score):
    fill_scores(place, data, score)
    row_parts, col_parts = [], []
    for t in range(2):
        top = score[t, 0]
        for b in range(1, BLOCKS):
            top = jnp.maximum(top, score[t, b])
        row_sum = jnp.zeros((ROWS, WIDE), f32)
        for b in range(BLOCKS):
            s = score[t, b]
            col_max = jnp.max(s, axis=0, keepdims=True)
            col_sum = jnp.sum(jnp.exp(s - col_max), axis=0, keepdims=True)
            col = col_max + jnp.log(col_sum)
            col_parts += [col[:, :128], col[:, 128:]]
            row_sum = row_sum + jnp.exp(s - top)
        top_t, sum_t = top.T, row_sum.T
        row_max = jnp.max(top_t, axis=0, keepdims=True)
        row_tot = jnp.sum(sum_t * jnp.exp(top_t - row_max), axis=0, keepdims=True)
        row = row_max + jnp.log(row_tot)
        row_parts += [row[:, q * 128 : (q + 1) * 128] for q in range(4)]
    out[...] = jnp.concatenate(row_parts + col_parts, axis=0)


def grad_kernel(place, data, parts, out, score, lse, high, low):
    fill_scores(place, data, score)
    for side in range(2):
        every = parts[side]
        top = jnp.max(every, axis=0)
        lse[side] = top + jnp.log(jnp.sum(jnp.exp(every - top[None]), axis=0))
    mine = lse[0, pl.ds(pl.multiple_of(place[0] * 8, 8), 8), :]
    for q in range(4):
        at = slice(q * 128, (q + 1) * 128)
        row = [jnp.broadcast_to(mine[t * 4 + q : t * 4 + q + 1], (128, 128)).T for t in range(2)]
        for b in range(BLOCKS):
            for h in range(2):
                prob = []
                for t in range(2):
                    s = score[t, b, at, h * 128 : (h + 1) * 128]
                    k = t * 8 + b * 2 + h
                    prob.append(jnp.exp(s - row[t]) + jnp.exp(s - lse[1, k : k + 1, :]))
                tile = prob[0] - prob[1]
                top_half = tile.astype(bf16)
                to = slice((2 * b + h) * 128, (2 * b + h + 1) * 128)
                high[at, to] = top_half
                low[at, to] = (tile - top_half.astype(f32)).astype(bf16)
    keys = jnp.concatenate([data[1, k, :, 0:256] for k in range(16)], axis=0)
    part = jnp.dot(high[...], keys, preferred_element_type=f32)
    part = (part + jnp.dot(low[...], keys, preferred_element_type=f32)).astype(bf16)
    for y in range(8):
        for half in range(2):
            out[2 * y + half] = part[y * HALF : (y + 1) * HALF, half * 128 : (half + 1) * 128]


VMEM = pl.BlockSpec(memory_space=pltpu.VMEM)
SMEM = pl.BlockSpec(memory_space=pltpu.SMEM)
SCORE = pltpu.VMEM((2, BLOCKS, ROWS, WIDE), f32)
PARAMS = pltpu.CompilerParams(vmem_limit_bytes=40 * 1024 * 1024)


def body(student, teacher):
    xh, z, y, xl, core = (lax.axis_index(a) for a in AXES)
    line = xh * 8 + z
    shift = jnp.where(core == xl, line % 4 * HALF, -4096)
    place = jnp.stack([core, y * HALF, line // 4, shift]).astype(jnp.int32)

    mine = jnp.concatenate([student.T, teacher.T], axis=0)
    own = lax.all_gather(mine, CHAN, axis=0, tiled=True)
    flipped = own.reshape(4, 2, 64, 128).transpose(3, 1, 0, 2).reshape(128, 512)
    share = lax.dynamic_slice_in_dim(flipped, xl * HALF, HALF, 0)
    got = mixed_exchange(jnp.broadcast_to(share[None], (16, HALF, 512)))
    data = lax.all_gather(got, "core", axis=0)

    stats = pl.pallas_call(
        stats_kernel,
        out_shape=jax.ShapeDtypeStruct((24, 128), f32),
        in_specs=[SMEM, VMEM],
        out_specs=VMEM,
        scratch_shapes=[SCORE],
        compiler_params=PARAMS,
    )(place, data)
    both = lax.all_gather(stats, "core", axis=0)
    rows = both[:, :8].reshape(16, 128)
    cols = jnp.logaddexp(both[0, 8:], both[1, 8:])
    pieces = jnp.where(core == 0, rows, cols)
    met = mixed_exchange(jnp.broadcast_to(pieces[None], (16, 16, 128)))
    parts = lax.all_gather(met, "core", axis=0)

    part = pl.pallas_call(
        grad_kernel,
        out_shape=jax.ShapeDtypeStruct((16, HALF, 128), bf16),
        in_specs=[SMEM, VMEM, VMEM],
        out_specs=VMEM,
        scratch_shapes=[
            SCORE,
            pltpu.VMEM((2, 16, 128), f32),
            pltpu.VMEM((ROWS, KEYS), bf16),
            pltpu.VMEM((ROWS, KEYS), bf16),
        ],
        compiler_params=PARAMS,
    )(place, data, parts)
    terms = lax.all_to_all(part, ("y", "xl"), split_axis=0, concat_axis=0)
    total = inverse_temp * jnp.sum(terms.astype(f32), axis=0)
    whole = lax.all_gather(total, "core", axis=0, tiled=True)
    return jnp.where(core == 0, whole[:, :64], whole[:, 64:])


def solution(mesh):
    split = Mesh(mesh.devices.reshape(SIZES), AXES)
    spec = P(("xh", "z", "y"), CHAN)
    return jax.shard_map(
        body, mesh=split, in_specs=(spec, spec), out_specs=spec, check_vma=False
    )
```

```python
import jax
import jax.numpy as jnp
from jax import lax
from jax.experimental import pallas as pl
from jax.experimental.pallas import tpu as pltpu
from jax.sharding import Mesh, PartitionSpec as P

inverse_temp = 0.125
AXES = ("xh", "z", "y", "xl", "core")
SIZES = (2, 8, 8, 2, 2)
CHAN = ("xl", "core")
HALF = 64
ROWS = 512
KEYS = 1024
WIDE = 256
BLOCKS = KEYS // WIDE
f32, bf16 = jnp.float32, jnp.bfloat16


def device(xh, z, y, xl, core):
    return (((xh * 8 + z) * 8 + y) * 2 + xl) * 2 + core


MIXED = [
    [device(xh, z, y, xl, 0) for y in range(8) for xl in range(2)] for xh in range(2) for z in range(8)
] + [[device(xh, z, y, xl, 1) for xh in range(2) for z in range(8)] for y in range(8) for xl in range(2)]


def mixed_exchange(pieces):
    return lax.all_to_all(pieces, AXES, split_axis=0, concat_axis=0, axis_index_groups=MIXED)


def share_kernel(place, own, out, turned):
    for t in range(2):
        turned[:, t * 256 : (t + 1) * 256] = jnp.concatenate(
            [own[c * 128 + t * 64 : c * 128 + (t + 1) * 64, :] for c in range(4)], axis=0
        ).T
    share = turned[pl.ds(pl.multiple_of(place[4], HALF), HALF), :]
    out[...] = jnp.broadcast_to(share[None], out.shape)


def by_core(place, own, other, run):
    @pl.when(place[0] == 0)
    def _():
        run(0, own, other)

    @pl.when(place[0] == 1)
    def _():
        run(1, other, own)


def fill_scores(place, core, row_data, key_data, score):
    for t in range(2):
        cut = slice(t * 256, (t + 1) * 256)
        rows = jnp.concatenate([row_data[2 * y + core, :, cut] for y in range(8)], axis=0)
        for b in range(BLOCKS):
            keys = jnp.concatenate([key_data[4 * b + k, :, cut] for k in range(4)], axis=0)
            score[t, b] = (
                lax.dot_general(rows, keys, (((1,), (1,)), ((), ())), preferred_element_type=f32)
                * inverse_temp
            )


def mask_self(place, score):
    first = pl.multiple_of(place[1], HALF)
    lane = lax.broadcasted_iota(jnp.int32, (HALF, WIDE), 1) - place[3]
    same = lane == lax.broadcasted_iota(jnp.int32, (HALF, WIDE), 0)
    for t in range(2):
        old = score[t, place[2], pl.ds(first, HALF), :]
        score[t, place[2], pl.ds(first, HALF), :] = jnp.where(same, -1e30, old)


def stats_kernel(place, own, other, out, score):
    by_core(place, own, other, lambda core, rows, keys: fill_scores(place, core, rows, keys, score))
    mask_self(place, score)
    row_parts, col_parts = [], []
    for t in range(2):
        top = score[t, 0]
        for b in range(1, BLOCKS):
            top = jnp.maximum(top, score[t, b])
        row_sum = jnp.zeros((ROWS, WIDE), f32)
        for b in range(BLOCKS):
            s = score[t, b]
            col_max = jnp.max(s, axis=0, keepdims=True)
            col_sum = jnp.sum(jnp.exp(s - col_max), axis=0, keepdims=True)
            col = col_max + jnp.log(col_sum)
            col_parts += [col[:, :128], col[:, 128:]]
            row_sum = row_sum + jnp.exp(s - top)
        top_t, sum_t = top.T, row_sum.T
        row_max = jnp.max(top_t, axis=0, keepdims=True)
        row_tot = jnp.sum(sum_t * jnp.exp(top_t - row_max), axis=0, keepdims=True)
        row = row_max + jnp.log(row_tot)
        row_parts += [row[:, q * 128 : (q + 1) * 128] for q in range(4)]
    out[...] = jnp.concatenate(row_parts + col_parts, axis=0)


def pieces_kernel(place, both, out):
    rows = jnp.concatenate([both[0, :8], both[1, :8]], axis=0)
    one, two = both[0, 8:], both[1, 8:]
    top = jnp.maximum(one, two)
    cols = top + jnp.log(jnp.exp(one - top) + jnp.exp(two - top))
    out[...] = jnp.broadcast_to(jnp.where(place[0] == 0, rows, cols)[None], out.shape)


def grad_kernel(place, own, other, parts, out, score, lse, high, low, students):
    def fill(core, row_data, key_data):
        fill_scores(place, core, row_data, key_data, score)
        for k in range(16):
            students[k * HALF : (k + 1) * HALF, :] = key_data[k, :, 0:256]

    by_core(place, own, other, fill)
    mask_self(place, score)
    for side in range(2):
        every = parts[side]
        top = jnp.max(every, axis=0)
        lse[side] = top + jnp.log(jnp.sum(jnp.exp(every - top[None]), axis=0))
    mine = lse[0, pl.ds(pl.multiple_of(place[0] * 8, 8), 8), :]
    for q in range(4):
        at = slice(q * 128, (q + 1) * 128)
        row = [jnp.broadcast_to(mine[t * 4 + q : t * 4 + q + 1], (128, 128)).T for t in range(2)]
        for b in range(BLOCKS):
            for h in range(2):
                prob = []
                for t in range(2):
                    s = score[t, b, at, h * 128 : (h + 1) * 128]
                    k = t * 8 + b * 2 + h
                    prob.append(jnp.exp(s - row[t]) + jnp.exp(s - lse[1, k : k + 1, :]))
                tile = prob[0] - prob[1]
                top_half = tile.astype(bf16)
                to = slice((2 * b + h) * 128, (2 * b + h + 1) * 128)
                high[at, to] = top_half
                low[at, to] = (tile - top_half.astype(f32)).astype(bf16)
    keys = students[...]
    part = jnp.dot(high[...], keys, preferred_element_type=f32)
    part = (part + jnp.dot(low[...], keys, preferred_element_type=f32)).astype(bf16)
    for y in range(8):
        for half in range(2):
            out[2 * y + half] = part[y * HALF : (y + 1) * HALF, half * 128 : (half + 1) * 128]


def sum_kernel(terms, out):
    total = terms[0].astype(f32)
    for k in range(1, 16):
        total = total + terms[k].astype(f32)
    out[...] = total * inverse_temp


def turn_kernel(place, whole, out, turned):
    turned[...] = whole[...].T
    out[...] = turned[pl.ds(pl.multiple_of(place[0] * 64, 64), 64), :]


VMEM = pl.BlockSpec(memory_space=pltpu.VMEM)
SMEM = pl.BlockSpec(memory_space=pltpu.SMEM)
SCORE = pltpu.VMEM((2, BLOCKS, ROWS, WIDE), f32)
PARAMS = pltpu.CompilerParams(vmem_limit_bytes=40 * 1024 * 1024)


def call(kernel, shape, dtype, *args, scratch=()):
    return pl.pallas_call(
        kernel,
        out_shape=jax.ShapeDtypeStruct(shape, dtype),
        in_specs=[SMEM if a.ndim == 1 else VMEM for a in args],
        out_specs=VMEM,
        scratch_shapes=list(scratch),
        compiler_params=PARAMS,
    )(*args)


def body(student, teacher):
    xh, z, y, xl, core = (lax.axis_index(a) for a in AXES)
    line = xh * 8 + z
    shift = jnp.where(core == xl, line % 4 * HALF, -4096)
    place = jnp.stack([core, y * HALF, line // 4, shift, xl * HALF]).astype(jnp.int32)

    mine = jnp.concatenate([student.T, teacher.T], axis=0)
    own = lax.all_gather(mine, CHAN, axis=0, tiled=True)
    share = call(share_kernel, (16, HALF, 512), bf16, place, own, scratch=[pltpu.VMEM((128, 512), bf16)])
    met = mixed_exchange(share)
    data = (met, lax.ppermute(met, "core", [(0, 1), (1, 0)]))

    stats = call(stats_kernel, (24, 128), f32, place, *data, scratch=[SCORE])
    pieces = call(pieces_kernel, (16, 16, 128), f32, place, lax.all_gather(stats, "core", axis=0))
    parts = lax.all_gather(mixed_exchange(pieces), "core", axis=0)

    wide = pltpu.VMEM((ROWS, KEYS), bf16)
    scratch = [SCORE, pltpu.VMEM((2, 16, 128), f32), wide, wide, pltpu.VMEM((KEYS, 256), bf16)]
    part = call(grad_kernel, (16, HALF, 128), bf16, place, *data, parts, scratch=scratch)
    terms = lax.all_to_all(part, ("y", "xl"), split_axis=0, concat_axis=0)
    total = call(sum_kernel, (HALF, 128), f32, terms)
    whole = lax.all_gather(total, "core", axis=0, tiled=True)
    return call(turn_kernel, (64, 128), f32, place, whole, scratch=[pltpu.VMEM((128, 128), f32)]).T


def solution(mesh):
    split = Mesh(mesh.devices.reshape(SIZES), AXES)
    spec = P(("xh", "z", "y"), CHAN)
    return jax.shard_map(
        body, mesh=split, in_specs=(spec, spec), out_specs=spec, check_vma=False
    )
```

```python
import jax
import jax.numpy as jnp
from jax import lax
from jax.experimental import pallas as pl
from jax.experimental.pallas import tpu as pltpu
from jax.sharding import Mesh, PartitionSpec as P

inverse_temp = 0.125
AXES = ("xh", "z", "y", "xl", "core")
SIZES = (2, 8, 8, 2, 2)
CHAN = ("xl", "core")
HALF = 64
ROWS = 512
KEYS = 1024
WIDE = 256
BLOCKS = KEYS // WIDE
f32, bf16 = jnp.float32, jnp.bfloat16


def device(xh, z, y, xl, core):
    return (((xh * 8 + z) * 8 + y) * 2 + xl) * 2 + core


MIXED = [
    [device(xh, z, y, xl, 0) for y in range(8) for xl in range(2)] for xh in range(2) for z in range(8)
] + [[device(xh, z, y, xl, 1) for xh in range(2) for z in range(8)] for y in range(8) for xl in range(2)]


def mixed_exchange(pieces):
    return lax.all_to_all(pieces, AXES, split_axis=0, concat_axis=0, axis_index_groups=MIXED)


def share_kernel(place, own, out, turned):
    for t in range(2):
        turned[:, t * 256 : (t + 1) * 256] = jnp.concatenate(
            [own[c * 128 + t * 64 : c * 128 + (t + 1) * 64, :] for c in range(4)], axis=0
        ).T
    share = turned[pl.ds(pl.multiple_of(place[4], HALF), HALF), :]
    out[...] = jnp.broadcast_to(share[None], out.shape)


def by_core(place, own, other, run):
    @pl.when(place[0] == 0)
    def _():
        run(0, own, other)

    @pl.when(place[0] == 1)
    def _():
        run(1, other, own)


def fill_scores(place, core, row_data, key_data, score):
    for t in range(2):
        cut = slice(t * 256, (t + 1) * 256)
        rows = jnp.concatenate([row_data[2 * y + core, :, cut] for y in range(8)], axis=0)
        for b in range(BLOCKS):
            keys = jnp.concatenate([key_data[4 * b + k, :, cut] for k in range(4)], axis=0)
            score[t, b] = (
                lax.dot_general(rows, keys, (((1,), (1,)), ((), ())), preferred_element_type=f32)
                * inverse_temp
            )


def mask_self(place, score):
    first = pl.multiple_of(place[1], HALF)
    lane = lax.broadcasted_iota(jnp.int32, (HALF, WIDE), 1) - place[3]
    same = lane == lax.broadcasted_iota(jnp.int32, (HALF, WIDE), 0)
    for t in range(2):
        old = score[t, place[2], pl.ds(first, HALF), :]
        score[t, place[2], pl.ds(first, HALF), :] = jnp.where(same, -1e30, old)


def stats_kernel(place, own, other, out, score):
    for t in range(2):
        cut = slice(t * 256, (t + 1) * 256)
        across = jnp.concatenate([other[k, :, cut] for k in range(16)], axis=0)
        for b in range(BLOCKS):
            items = jnp.concatenate([own[4 * b + k, :, cut] for k in range(4)], axis=0)
            score[t, b] = (
                lax.dot_general(across, items, (((1,), (1,)), ((), ())), preferred_element_type=f32)
                * inverse_temp
            )
    first = pl.multiple_of(place[5], HALF)
    lane = lax.broadcasted_iota(jnp.int32, (HALF, WIDE), 1) - place[7]
    same = lane == lax.broadcasted_iota(jnp.int32, (HALF, WIDE), 0)
    for t in range(2):
        old = score[t, place[6], pl.ds(first, HALF), :]
        score[t, place[6], pl.ds(first, HALF), :] = jnp.where(same, -1e30, old)
    parts = []
    for t in range(2):
        for b in range(BLOCKS):
            s = score[t, b]
            top = jnp.max(s, axis=0, keepdims=True)
            part = top + jnp.log(jnp.sum(jnp.exp(s - top), axis=0, keepdims=True))
            parts += [part[:, :128], part[:, 128:]]
    out[...] = jnp.broadcast_to(jnp.concatenate(parts, axis=0)[None], out.shape)


def grad_kernel(place, own, other, parts, out, score, lse, high, low, students):
    def fill(core, row_data, key_data):
        fill_scores(place, core, row_data, key_data, score)
        for k in range(16):
            students[k * HALF : (k + 1) * HALF, :] = key_data[k, :, 0:256]

    by_core(place, own, other, fill)
    mask_self(place, score)
    for side in range(2):
        every = parts[side]
        top = jnp.max(every, axis=0)
        lse[side] = top + jnp.log(jnp.sum(jnp.exp(every - top[None]), axis=0))

    def half(k):
        one, two = lse[0, k : k + 1, :], lse[0, k + 1 : k + 2, :]
        low_half = jnp.concatenate([one[:, :HALF], two[:, :HALF]], axis=1)
        high_half = jnp.concatenate([one[:, HALF:], two[:, HALF:]], axis=1)
        return jnp.where(place[0] == 0, low_half, high_half)

    for q in range(4):
        at = slice(q * 128, (q + 1) * 128)
        row = [jnp.broadcast_to(half(t * 8 + 2 * q), (128, 128)).T for t in range(2)]
        for b in range(BLOCKS):
            for h in range(2):
                prob = []
                for t in range(2):
                    s = score[t, b, at, h * 128 : (h + 1) * 128]
                    k = t * 8 + b * 2 + h
                    prob.append(jnp.exp(s - row[t]) + jnp.exp(s - lse[1, k : k + 1, :]))
                tile = prob[0] - prob[1]
                top_half = tile.astype(bf16)
                to = slice((2 * b + h) * 128, (2 * b + h + 1) * 128)
                high[at, to] = top_half
                low[at, to] = (tile - top_half.astype(f32)).astype(bf16)
    keys = students[...]
    part = jnp.dot(high[...], keys, preferred_element_type=f32)
    part = (part + jnp.dot(low[...], keys, preferred_element_type=f32)).astype(bf16)
    for y in range(8):
        for half in range(2):
            out[2 * y + half] = part[y * HALF : (y + 1) * HALF, half * 128 : (half + 1) * 128]


def sum_kernel(terms, out):
    total = terms[0].astype(f32)
    for k in range(1, 16):
        total = total + terms[k].astype(f32)
    out[...] = total * inverse_temp


def turn_kernel(place, whole, out, turned):
    turned[...] = whole[...].T
    out[...] = turned[pl.ds(pl.multiple_of(place[0] * 64, 64), 64), :]


VMEM = pl.BlockSpec(memory_space=pltpu.VMEM)
SMEM = pl.BlockSpec(memory_space=pltpu.SMEM)
SCORE = pltpu.VMEM((2, BLOCKS, ROWS, WIDE), f32)
PARAMS = pltpu.CompilerParams(vmem_limit_bytes=40 * 1024 * 1024)


def call(kernel, shape, dtype, *args, scratch=()):
    return pl.pallas_call(
        kernel,
        out_shape=jax.ShapeDtypeStruct(shape, dtype),
        in_specs=[SMEM if a.ndim == 1 else VMEM for a in args],
        out_specs=VMEM,
        scratch_shapes=list(scratch),
        compiler_params=PARAMS,
    )(*args)


def body(student, teacher):
    xh, z, y, xl, core = (lax.axis_index(a) for a in AXES)
    line = xh * 8 + z
    shift = jnp.where(core == xl, line % 4 * HALF, -4096)
    block = 2 * y + xl
    mine_at, other_at = jnp.where(core == 0, block, line), jnp.where(core == 0, line, block)
    place = jnp.stack(
        [core, y * HALF, line // 4, shift, xl * HALF, other_at * HALF, mine_at // 4, mine_at % 4 * HALF]
    ).astype(jnp.int32)

    mine = jnp.concatenate([student.T, teacher.T], axis=0)
    own = lax.all_gather(mine, CHAN, axis=0, tiled=True)
    share = call(share_kernel, (16, HALF, 512), bf16, place, own, scratch=[pltpu.VMEM((128, 512), bf16)])
    met = mixed_exchange(share)
    data = (met, lax.ppermute(met, "core", [(0, 1), (1, 0)]))

    tile = pltpu.VMEM((2, BLOCKS, KEYS, WIDE), f32)
    pieces = call(stats_kernel, (16, 16, 128), f32, place, *data, scratch=[tile])
    parts = lax.all_gather(mixed_exchange(pieces), "core", axis=0)

    wide = pltpu.VMEM((ROWS, KEYS), bf16)
    scratch = [SCORE, pltpu.VMEM((2, 16, 128), f32), wide, wide, pltpu.VMEM((KEYS, 256), bf16)]
    part = call(grad_kernel, (16, HALF, 128), bf16, place, *data, parts, scratch=scratch)
    terms = lax.all_to_all(part, ("y", "xl"), split_axis=0, concat_axis=0)
    total = call(sum_kernel, (HALF, 128), f32, terms)
    whole = lax.all_gather(total, "core", axis=0, tiled=True)
    return call(turn_kernel, (64, 128), f32, place, whole, scratch=[pltpu.VMEM((128, 128), f32)]).T


def solution(mesh):
    split = Mesh(mesh.devices.reshape(SIZES), AXES)
    spec = P(("xh", "z", "y"), CHAN)
    return jax.shard_map(
        body, mesh=split, in_specs=(spec, spec), out_specs=spec, check_vma=False
    )
```

```python
import jax
import jax.numpy as jnp
from jax import lax
from jax.experimental import pallas as pl
from jax.experimental.pallas import tpu as pltpu
from jax.sharding import Mesh, PartitionSpec as P

inverse_temp = 0.125
AXES = ("xh", "z", "y", "xl", "core")
SIZES = (2, 8, 8, 2, 2)
CHAN = ("xl", "core")
HALF = 64
ROWS = 512
KEYS = 1024
WIDE = 256
BLOCKS = KEYS // WIDE
f32, bf16 = jnp.float32, jnp.bfloat16


def device(xh, z, y, xl, core):
    return (((xh * 8 + z) * 8 + y) * 2 + xl) * 2 + core


MIXED = [
    [device(xh, z, y, xl, 0) for y in range(8) for xl in range(2)] for xh in range(2) for z in range(8)
] + [[device(xh, z, y, xl, 1) for xh in range(2) for z in range(8)] for y in range(8) for xl in range(2)]


def mixed_exchange(pieces):
    return lax.all_to_all(pieces, AXES, split_axis=0, concat_axis=0, axis_index_groups=MIXED)


def position():
    xh, z, y, xl, core = (lax.axis_index(a) for a in AXES)
    line = xh * 8 + z
    shift = jnp.where(core == xl, line % 4 * HALF, -4096)
    block = 2 * y + xl
    mine_at, other_at = jnp.where(core == 0, block, line), jnp.where(core == 0, line, block)
    return (
        core, y * HALF, line // 4, shift, xl * HALF, other_at * HALF, mine_at // 4, mine_at % 4 * HALF,
    )


def share_kernel(own, out, turned):
    place = position()
    for t in range(2):
        turned[:, t * 256 : (t + 1) * 256] = jnp.concatenate(
            [own[c * 128 + t * 64 : c * 128 + (t + 1) * 64, :] for c in range(4)], axis=0
        ).T
    share = turned[pl.ds(pl.multiple_of(place[4], HALF), HALF), :]
    out[...] = jnp.broadcast_to(share[None], out.shape)


def by_core(place, own, other, run):
    @pl.when(place[0] == 0)
    def _():
        run(0, own, other)

    @pl.when(place[0] == 1)
    def _():
        run(1, other, own)


def fill_scores(place, core, row_data, key_data, score):
    for t in range(2):
        cut = slice(t * 256, (t + 1) * 256)
        rows = jnp.concatenate([row_data[2 * y + core, :, cut] for y in range(8)], axis=0)
        for b in range(BLOCKS):
            keys = jnp.concatenate([key_data[4 * b + k, :, cut] for k in range(4)], axis=0)
            score[t, b] = (
                lax.dot_general(rows, keys, (((1,), (1,)), ((), ())), preferred_element_type=f32)
                * inverse_temp
            )


def mask_self(place, score):
    first = pl.multiple_of(place[1], HALF)
    lane = lax.broadcasted_iota(jnp.int32, (HALF, WIDE), 1) - place[3]
    same = lane == lax.broadcasted_iota(jnp.int32, (HALF, WIDE), 0)
    for t in range(2):
        old = score[t, place[2], pl.ds(first, HALF), :]
        score[t, place[2], pl.ds(first, HALF), :] = jnp.where(same, -1e30, old)


def stats_kernel(own, other, out, score):
    place = position()
    for t in range(2):
        cut = slice(t * 256, (t + 1) * 256)
        across = jnp.concatenate([other[k, :, cut] for k in range(16)], axis=0)
        for b in range(BLOCKS):
            items = jnp.concatenate([own[4 * b + k, :, cut] for k in range(4)], axis=0)
            score[t, b] = (
                lax.dot_general(across, items, (((1,), (1,)), ((), ())), preferred_element_type=f32)
                * inverse_temp
            )
    first = pl.multiple_of(place[5], HALF)
    lane = lax.broadcasted_iota(jnp.int32, (HALF, WIDE), 1) - place[7]
    same = lane == lax.broadcasted_iota(jnp.int32, (HALF, WIDE), 0)
    for t in range(2):
        old = score[t, place[6], pl.ds(first, HALF), :]
        score[t, place[6], pl.ds(first, HALF), :] = jnp.where(same, -1e30, old)
    parts = []
    for t in range(2):
        for b in range(BLOCKS):
            s = score[t, b]
            top = jnp.max(s, axis=0, keepdims=True)
            part = top + jnp.log(jnp.sum(jnp.exp(s - top), axis=0, keepdims=True))
            parts += [part[:, :128], part[:, 128:]]
    out[...] = jnp.broadcast_to(jnp.concatenate(parts, axis=0)[None], out.shape)


def grad_kernel(own, other, parts, out, score, lse, high, low, students):
    place = position()

    def fill(core, row_data, key_data):
        fill_scores(place, core, row_data, key_data, score)
        for k in range(16):
            students[k * HALF : (k + 1) * HALF, :] = key_data[k, :, 0:256]

    by_core(place, own, other, fill)
    mask_self(place, score)
    for side in range(2):
        every = parts[side]
        top = jnp.max(every, axis=0)
        lse[side] = top + jnp.log(jnp.sum(jnp.exp(every - top[None]), axis=0))

    def half(k):
        one, two = lse[0, k : k + 1, :], lse[0, k + 1 : k + 2, :]
        low_half = jnp.concatenate([one[:, :HALF], two[:, :HALF]], axis=1)
        high_half = jnp.concatenate([one[:, HALF:], two[:, HALF:]], axis=1)
        return jnp.where(place[0] == 0, low_half, high_half)

    for q in range(4):
        at = slice(q * 128, (q + 1) * 128)
        row = [jnp.broadcast_to(half(t * 8 + 2 * q), (128, 128)).T for t in range(2)]
        for b in range(BLOCKS):
            for h in range(2):
                prob = []
                for t in range(2):
                    s = score[t, b, at, h * 128 : (h + 1) * 128]
                    k = t * 8 + b * 2 + h
                    prob.append(jnp.exp(s - row[t]) + jnp.exp(s - lse[1, k : k + 1, :]))
                tile = prob[0] - prob[1]
                top_half = tile.astype(bf16)
                to = slice((2 * b + h) * 128, (2 * b + h + 1) * 128)
                high[at, to] = top_half
                low[at, to] = (tile - top_half.astype(f32)).astype(bf16)
    keys = students[...]
    part = jnp.dot(high[...], keys, preferred_element_type=f32)
    part = (part + jnp.dot(low[...], keys, preferred_element_type=f32)).astype(bf16)
    for y in range(8):
        for half in range(2):
            out[2 * y + half] = part[y * HALF : (y + 1) * HALF, half * 128 : (half + 1) * 128]


def sum_kernel(terms, out):
    total = terms[0].astype(f32)
    for k in range(1, 16):
        total = total + terms[k].astype(f32)
    out[...] = total * inverse_temp


def turn_kernel(whole, out, turned):
    place = position()
    turned[...] = whole[...].T
    out[...] = turned[pl.ds(pl.multiple_of(place[0] * 64, 64), 64), :]


VMEM = pl.BlockSpec(memory_space=pltpu.VMEM)
SMEM = pl.BlockSpec(memory_space=pltpu.SMEM)
SCORE = pltpu.VMEM((2, BLOCKS, ROWS, WIDE), f32)
PARAMS = pltpu.CompilerParams(vmem_limit_bytes=40 * 1024 * 1024)


def call(kernel, shape, dtype, *args, scratch=()):
    return pl.pallas_call(
        kernel,
        out_shape=jax.ShapeDtypeStruct(shape, dtype),
        in_specs=[SMEM if a.ndim == 1 else VMEM for a in args],
        out_specs=VMEM,
        scratch_shapes=list(scratch),
        compiler_params=PARAMS,
    )(*args)


def body(student, teacher):
    mine = jnp.concatenate([student.T, teacher.T], axis=0)
    own = lax.all_gather(mine, CHAN, axis=0, tiled=True)
    share = call(share_kernel, (16, HALF, 512), bf16, own, scratch=[pltpu.VMEM((128, 512), bf16)])
    met = mixed_exchange(share)
    data = (met, lax.ppermute(met, "core", [(0, 1), (1, 0)]))

    tile = pltpu.VMEM((2, BLOCKS, KEYS, WIDE), f32)
    pieces = call(stats_kernel, (16, 16, 128), f32, *data, scratch=[tile])
    parts = lax.all_gather(mixed_exchange(pieces), "core", axis=0)

    wide = pltpu.VMEM((ROWS, KEYS), bf16)
    scratch = [SCORE, pltpu.VMEM((2, 16, 128), f32), wide, wide, pltpu.VMEM((KEYS, 256), bf16)]
    part = call(grad_kernel, (16, HALF, 128), bf16, *data, parts, scratch=scratch)
    terms = lax.all_to_all(part, ("y", "xl"), split_axis=0, concat_axis=0)
    total = call(sum_kernel, (HALF, 128), f32, terms)
    whole = lax.all_gather(total, "core", axis=0, tiled=True)
    return call(turn_kernel, (64, 128), f32, whole, scratch=[pltpu.VMEM((128, 128), f32)]).T


def solution(mesh):
    split = Mesh(mesh.devices.reshape(SIZES), AXES)
    spec = P(("xh", "z", "y"), CHAN)
    return jax.shard_map(
        body, mesh=split, in_specs=(spec, spec), out_specs=spec, check_vma=False
    )
```

```python
import jax
import jax.numpy as jnp
from jax import lax
from jax.experimental import pallas as pl
from jax.experimental.pallas import tpu as pltpu
from jax.sharding import Mesh, PartitionSpec as P

inverse_temp = 0.125
AXES = ("xh", "z", "y", "xl", "core")
SIZES = (2, 8, 8, 2, 2)
CHAN = ("xl", "core")
HALF = 64
ROWS = 512
KEYS = 1024
WIDE = 256
BLOCKS = KEYS // WIDE
f32, bf16 = jnp.float32, jnp.bfloat16


def device(xh, z, y, xl, core):
    return (((xh * 8 + z) * 8 + y) * 2 + xl) * 2 + core


MIXED = [
    [device(xh, z, y, xl, 0) for y in range(8) for xl in range(2)] for xh in range(2) for z in range(8)
] + [[device(xh, z, y, xl, 1) for xh in range(2) for z in range(8)] for y in range(8) for xl in range(2)]


def mixed_exchange(pieces):
    return lax.all_to_all(pieces, AXES, split_axis=0, concat_axis=0, axis_index_groups=MIXED)


def position():
    xh, z, y, xl, core = (lax.axis_index(a) for a in AXES)
    line = xh * 8 + z
    shift = jnp.where(core == xl, line % 4 * HALF, -4096)
    block = 2 * y + xl
    mine_at, other_at = jnp.where(core == 0, block, line), jnp.where(core == 0, line, block)
    return (
        core, y * HALF, line // 4, shift, xl * HALF, other_at * HALF, mine_at // 4, mine_at % 4 * HALF,
    )


def share_kernel(own, out, turned):
    place = position()
    for t in range(2):
        turned[:, t * 256 : (t + 1) * 256] = jnp.concatenate(
            [own[c * 128 + t * 64 : c * 128 + (t + 1) * 64, :] for c in range(4)], axis=0
        ).T
    share = turned[pl.ds(pl.multiple_of(place[4], HALF), HALF), :]
    out[...] = jnp.broadcast_to(share[None], out.shape)


def by_core(place, own, other, run):
    @pl.when(place[0] == 0)
    def _():
        run(0, own, other)

    @pl.when(place[0] == 1)
    def _():
        run(1, other, own)


def fill_scores(place, core, row_data, key_data, score):
    for t in range(2):
        cut = slice(t * 256, (t + 1) * 256)
        rows = jnp.concatenate([row_data[2 * y + core, :, cut] for y in range(8)], axis=0)
        for b in range(BLOCKS):
            keys = jnp.concatenate([key_data[4 * b + k, :, cut] for k in range(4)], axis=0)
            score[t, b] = scaled_product(rows, keys)


def mask_self(place, score):
    first = pl.multiple_of(place[1], HALF)
    lane = lax.broadcasted_iota(jnp.int32, (HALF, WIDE), 1) - place[3]
    same = lane == lax.broadcasted_iota(jnp.int32, (HALF, WIDE), 0)
    for t in range(2):
        old = score[t, place[2], pl.ds(first, HALF), :]
        score[t, place[2], pl.ds(first, HALF), :] = jnp.where(same, -1e30, old)


def mask_chunk(chunk, first, shift, wanted):
    at = pl.ds(pl.multiple_of(first, HALF), HALF)
    lane = lax.broadcasted_iota(jnp.int32, (HALF, WIDE), 1) - jnp.where(wanted, shift, -4096)
    same = lane == lax.broadcasted_iota(jnp.int32, (HALF, WIDE), 0)
    chunk[at, :] = jnp.where(same, -1e30, chunk[at, :])


def scaled_product(left, right):
    scores = lax.dot_general(left, right, (((1,), (1,)), ((), ())), preferred_element_type=f32)
    return scores * inverse_temp


def stats_kernel(own, other, out, *score):
    place = position()
    chunks = [(t, b) for t in range(2) for b in range(BLOCKS)]
    across = [
        jnp.concatenate([other[k, :, t * 256 : (t + 1) * 256] for k in range(16)], axis=0) for t in range(2)
    ]

    def fill(n):
        t, b = chunks[n]
        items = jnp.concatenate(
            [own[4 * b + k, :, t * 256 : (t + 1) * 256] for k in range(4)], axis=0
        )
        score[n][...] = scaled_product(across[t], items)
        mask_chunk(score[n], place[5], place[7], place[6] == b)

    parts = []
    fill(0)
    for n in range(len(chunks)):
        if n + 1 < len(chunks):
            fill(n + 1)
        s = score[n][...]
        top = jnp.max(s, axis=0, keepdims=True)
        part = top + jnp.log(jnp.sum(jnp.exp(s - top), axis=0, keepdims=True))
        parts += [part[:, :128], part[:, 128:]]
    out[...] = jnp.broadcast_to(jnp.concatenate(parts, axis=0)[None], out.shape)


def grad_kernel(own, other, parts, out, score, lse, high, low, students):
    place = position()

    def fill(core, row_data, key_data):
        fill_scores(place, core, row_data, key_data, score)
        for k in range(16):
            students[k * HALF : (k + 1) * HALF, :] = key_data[k, :, 0:256]

    by_core(place, own, other, fill)
    mask_self(place, score)
    for side in range(2):
        every = parts[side]
        top = jnp.max(every, axis=0)
        lse[side] = top + jnp.log(jnp.sum(jnp.exp(every - top[None]), axis=0))

    def half(k):
        one, two = lse[0, k : k + 1, :], lse[0, k + 1 : k + 2, :]
        low_half = jnp.concatenate([one[:, :HALF], two[:, :HALF]], axis=1)
        high_half = jnp.concatenate([one[:, HALF:], two[:, HALF:]], axis=1)
        return jnp.where(place[0] == 0, low_half, high_half)

    for q in range(4):
        at = slice(q * 128, (q + 1) * 128)
        row = [jnp.broadcast_to(half(t * 8 + 2 * q), (128, 128)).T for t in range(2)]
        for b in range(BLOCKS):
            for h in range(2):
                prob = []
                for t in range(2):
                    s = score[t, b, at, h * 128 : (h + 1) * 128]
                    k = t * 8 + b * 2 + h
                    prob.append(jnp.exp(s - row[t]) + jnp.exp(s - lse[1, k : k + 1, :]))
                tile = prob[0] - prob[1]
                top_half = tile.astype(bf16)
                to = slice((2 * b + h) * 128, (2 * b + h + 1) * 128)
                high[at, to] = top_half
                low[at, to] = (tile - top_half.astype(f32)).astype(bf16)
    keys = students[...]
    part = jnp.dot(high[...], keys, preferred_element_type=f32)
    part = part + jnp.dot(low[...], keys, preferred_element_type=f32)
    for y in range(8):
        for half in range(2):
            block = part[y * HALF : (y + 1) * HALF, half * 128 : (half + 1) * 128]
            one, two = block[:32], block[32:]
            for c in range(2):
                at = slice(c * 64, (c + 1) * 64)
                piece = jnp.concatenate([one[:, at], two[:, at]], axis=1)
                out[4 * y + 2 * half + c] = piece.astype(bf16)


def sum_kernel(terms, out):
    halves = []
    for k in range(2):
        total = terms[k].astype(f32)
        for n in range(1, 16):
            total = total + terms[2 * n + k].astype(f32)
        halves.append(total)
    turned = (jnp.concatenate(halves, axis=0) * inverse_temp).T
    out[...] = jnp.concatenate(
        [turned[g * 64 : (g + 1) * 64, k * 32 : (k + 1) * 32] for k in range(2) for g in range(2)], axis=1
    )


VMEM = pl.BlockSpec(memory_space=pltpu.VMEM)
SCORE = pltpu.VMEM((2, BLOCKS, ROWS, WIDE), f32)
PARAMS = pltpu.CompilerParams(vmem_limit_bytes=40 * 1024 * 1024)


def call(kernel, shape, dtype, *args, scratch=()):
    return pl.pallas_call(
        kernel,
        out_shape=jax.ShapeDtypeStruct(shape, dtype),
        in_specs=[VMEM] * len(args),
        out_specs=VMEM,
        scratch_shapes=list(scratch),
        compiler_params=PARAMS,
    )(*args)


def body(student, teacher):
    mine = jnp.concatenate([student.T, teacher.T], axis=0)
    own = lax.all_gather(mine, CHAN, axis=0, tiled=True)
    share = call(share_kernel, (16, HALF, 512), bf16, own, scratch=[pltpu.VMEM((128, 512), bf16)])
    met = mixed_exchange(share)
    data = (met, lax.ppermute(met, "core", [(0, 1), (1, 0)]))

    tiles = [pltpu.VMEM((KEYS, WIDE), f32)] * (2 * BLOCKS)
    pieces = call(stats_kernel, (16, 16, 128), f32, *data, scratch=tiles)
    parts = lax.all_gather(mixed_exchange(pieces), "core", axis=0)

    wide = pltpu.VMEM((ROWS, KEYS), bf16)
    scratch = [SCORE, pltpu.VMEM((2, 16, 128), f32), wide, wide, pltpu.VMEM((KEYS, 256), bf16)]
    part = call(grad_kernel, (32, 32, 128), bf16, *data, parts, scratch=scratch)
    terms = lax.all_to_all(part, ("y", "xl", "core"), split_axis=0, concat_axis=0)
    return call(sum_kernel, (64, 128), f32, terms).T


def solution(mesh):
    split = Mesh(mesh.devices.reshape(SIZES), AXES)
    spec = P(("xh", "z", "y"), CHAN)
    return jax.shard_map(
        body, mesh=split, in_specs=(spec, spec), out_specs=spec, check_vma=False
    )
```

```python
import jax
import jax.numpy as jnp
from jax import lax
from jax.experimental import pallas as pl
from jax.experimental.pallas import tpu as pltpu
from jax.sharding import Mesh, PartitionSpec as P

inverse_temp = 0.125
AXES = ("xh", "z", "y", "xl", "core")
SIZES = (2, 8, 8, 2, 2)
CHAN = ("xl", "core")
HALF = 64
ROWS = 512
KEYS = 1024
WIDE = 256
BLOCKS = KEYS // WIDE
PART = 32
f32, bf16 = jnp.float32, jnp.bfloat16


def device(xh, z, y, xl, core):
    return (((xh * 8 + z) * 8 + y) * 2 + xl) * 2 + core


MIXED = [
    [device(xh, z, y, xl, 0) for y in range(8) for xl in range(2)] for xh in range(2) for z in range(8)
] + [[device(xh, z, y, xl, 1) for xh in range(2) for z in range(8)] for y in range(8) for xl in range(2)]


WIDER = [
    [device(xh, z, y, xl, 0) for y in range(8) for xh in range(2) for xl in range(2)] for z in range(8)
] + [[device(xh, z, y, xl, 1) for z in range(8) for xh in range(2) for xl in range(2)] for y in range(8)]


def mixed_exchange(pieces, groups):
    return lax.all_to_all(pieces, AXES, split_axis=0, concat_axis=0, axis_index_groups=groups)


def position():
    xh, z, y, xl, core = (lax.axis_index(a) for a in AXES)
    first = core == 0
    return core, jnp.where(first, y, z), jnp.where(first, z, y), xh == xl


def share_kernel(mine, out, turned):
    core = lax.axis_index("core")
    for t in range(2):
        turned[:, t * 128 : (t + 1) * 128] = jnp.concatenate(
            [mine[c * 128 + t * 64 : c * 128 + (t + 1) * 64, :] for c in range(2)], axis=0
        ).T
    for k in range(4):
        half = jnp.where(core == 0, k // 2, k % 2)
        share = turned[pl.ds(pl.multiple_of(half * HALF, HALF), HALF), :]
        for n in range(8):
            out[4 * n + k] = share


def block(data, n, t, at=slice(None)):
    cut = slice(t * 128, (t + 1) * 128)
    return jnp.concatenate([data[2 * n, at, cut], data[2 * n + 1, at, cut]], axis=1)


def blocks(data, first, count, t, at=slice(None)):
    return jnp.concatenate([block(data, first + k, t, at) for k in range(count)], axis=0)


def mask_chunk(chunk, first, shift, wanted):
    at = pl.ds(pl.multiple_of(first, HALF), HALF)
    lane = lax.broadcasted_iota(jnp.int32, (HALF, WIDE), 1) - jnp.where(wanted, shift, -4096)
    same = lane == lax.broadcasted_iota(jnp.int32, (HALF, WIDE), 0)
    chunk[at, :] = jnp.where(same, -1e30, chunk[at, :])


def scaled_product(left, right):
    scores = lax.dot_general(left, right, (((1,), (1,)), ((), ())), preferred_element_type=f32)
    return scores * inverse_temp


def stats_kernel(own, other, out, *score):
    core, line, other_line, overlaps = position()
    chunks = [(t, b) for t in range(2) for b in range(BLOCKS)]
    across = [blocks(other, 0, 16, t) for t in range(2)]

    def fill(n):
        t, b = chunks[n]
        score[n][...] = scaled_product(across[t], blocks(own, 4 * b, 4, t))
        for e in range(2):
            mask_chunk(
                score[n],
                (2 * other_line + e) * HALF,
                line % 2 * 128 + e * HALF,
                jnp.logical_and(overlaps, line // 2 == b),
            )

    parts = []
    fill(0)
    for n in range(len(chunks)):
        if n + 1 < len(chunks):
            fill(n + 1)
        s = score[n][...]
        top = jnp.max(s, axis=0, keepdims=True)
        part = top + jnp.log(jnp.sum(jnp.exp(s - top), axis=0, keepdims=True))
        parts += [part[:, :128], part[:, 128:]]
    out[...] = jnp.broadcast_to(jnp.concatenate(parts, axis=0)[None], out.shape)


def grad_kernel(own, other, parts, out, score, lse, high, low, picked_rows, students):
    core, line, other_line, overlaps = position()
    at_core = pl.ds(pl.multiple_of(core * PART, PART), PART)
    @pl.when(core < 2)
    def _():
        for n in range(16):
            to = slice(n * PART, (n + 1) * PART)
            for half in range(2):
                for t in range(2):
                    cut, at = slice(t * 128, (t + 1) * 128), slice(half * 128, (half + 1) * 128)
                    picked_rows[t, to, at] = own[2 * n + half, at_core, cut]
                    students[t, n * HALF : (n + 1) * HALF, at] = other[2 * n + half, :, cut]
        for t in range(2):
            rows = picked_rows[t]
            for b in range(BLOCKS):
                score[t, b] = scaled_product(rows, students[t, b * WIDE : (b + 1) * WIDE, :])

    for side in range(2):
        every = parts[side]
        top = jnp.max(every, axis=0)
        lse[side] = top + jnp.log(jnp.sum(jnp.exp(every - top[None]), axis=0))
    lane = lax.broadcasted_iota(jnp.int32, (PART, WIDE), 1)
    item = lax.broadcasted_iota(jnp.int32, (PART, WIDE), 0)
    for e in range(2):
        shift = jnp.where(overlaps, other_line % 2 * 128 + e * HALF + core * PART, -4096)
        same = lane - shift == item
        at = pl.ds(pl.multiple_of((2 * line + e) * PART, PART), PART)
        for t in range(2):
            old = score[t, other_line // 2, at, :]
            score[t, other_line // 2, at, :] = jnp.where(same, -1e30, old)
    mine, others = lse[core], lse[1 - core]

    def of_part(k):
        picked = []
        for c in range(2):
            starts = [e * HALF + c * PART for e in range(2)]
            picked.append(
                jnp.concatenate(
                    [mine[k + d : k + d + 1, at : at + PART] for d in range(2) for at in starts], axis=1
                )
            )
        return jnp.where(core == 0, picked[0], picked[1])

    for q in range(4):
        at = slice(q * 128, (q + 1) * 128)
        row = [jnp.broadcast_to(of_part(t * 8 + 2 * q), (128, 128)).T for t in range(2)]
        for b in range(BLOCKS):
            for h in range(2):
                prob = []
                for t in range(2):
                    s = score[t, b, at, h * 128 : (h + 1) * 128]
                    k = t * 8 + b * 2 + h
                    prob.append(jnp.exp(s - row[t]) + jnp.exp(s - others[k : k + 1, :]))
                tile = prob[0] - prob[1]
                top_half = tile.astype(bf16)
                to = slice((2 * b + h) * 128, (2 * b + h + 1) * 128)
                high[at, to] = top_half
                low[at, to] = (tile - top_half.astype(f32)).astype(bf16)
    part = jnp.dot(high[...], students[0], preferred_element_type=f32)
    part = (part + jnp.dot(low[...], students[0], preferred_element_type=f32)).astype(bf16)
    for n in range(16):
        for half in range(2):
            out[2 * n + half] = part[n * PART : (n + 1) * PART, half * 128 : (half + 1) * 128]


def sum_kernel(terms, out):
    first = lax.axis_index("core") == 0
    sums = []
    for k in range(4):
        total = terms[k].astype(f32)
        for n in range(1, 8):
            total = total + terms[4 * n + k].astype(f32)
        sums.append(total * inverse_temp)
    out[:PART] = sums[0] + jnp.where(first, sums[1], sums[2])
    out[PART:] = sums[3] + jnp.where(first, sums[2], sums[1])


def turn_kernel(whole, out, turned):
    parts = [whole[k * 64 + half * PART : k * 64 + (half + 1) * PART] for half in range(2) for k in range(2)]
    turned[...] = jnp.concatenate(parts, axis=0).T
    out[...] = turned[pl.ds(pl.multiple_of(lax.axis_index("core") * 64, 64), 64), :]


VMEM = pl.BlockSpec(memory_space=pltpu.VMEM)
PARAMS = pltpu.CompilerParams(vmem_limit_bytes=40 * 1024 * 1024)


def call(kernel, shape, dtype, *args, scratch=()):
    return pl.pallas_call(
        kernel,
        out_shape=jax.ShapeDtypeStruct(shape, dtype),
        in_specs=[VMEM] * len(args),
        out_specs=VMEM,
        scratch_shapes=list(scratch),
        compiler_params=PARAMS,
    )(*args)


def body(student, teacher):
    mine = jnp.concatenate([student.T, teacher.T], axis=0)
    chip = lax.all_gather(mine, "core", axis=0, tiled=True)
    share = call(share_kernel, (32, HALF, 256), bf16, chip, scratch=[pltpu.VMEM((128, 256), bf16)])
    own = mixed_exchange(share, WIDER)
    other = lax.ppermute(own, "core", [(0, 1), (1, 0)])

    tiles = [pltpu.VMEM((KEYS, WIDE), f32)] * (2 * BLOCKS)
    pieces = call(stats_kernel, (16, 16, 128), f32, own, other, scratch=tiles)
    parts = lax.all_gather(mixed_exchange(pieces, MIXED), "core", axis=0)

    wide = pltpu.VMEM((ROWS, KEYS), bf16)
    scratch = [pltpu.VMEM((2, BLOCKS, ROWS, WIDE), f32), pltpu.VMEM((2, 16, 128), f32), wide, wide]
    scratch += [pltpu.VMEM((2, ROWS, 256), bf16), pltpu.VMEM((2, KEYS, 256), bf16)]
    part = call(grad_kernel, (32, PART, 128), bf16, own, other, parts, scratch=scratch)
    terms = mixed_exchange(part, WIDER)
    total = call(sum_kernel, (HALF, 128), f32, terms)
    whole = lax.all_gather(total, "core", axis=0, tiled=True)
    return call(turn_kernel, (64, 128), f32, whole, scratch=[pltpu.VMEM((128, 128), f32)]).T


def solution(mesh):
    split = Mesh(mesh.devices.reshape(SIZES), AXES)
    spec = P(("xh", "z", "y"), CHAN)
    return jax.shard_map(
        body, mesh=split, in_specs=(spec, spec), out_specs=spec, check_vma=False
    )
```

```python
import jax
import jax.numpy as jnp
from jax import lax
from jax.experimental import pallas as pl
from jax.experimental.pallas import tpu as pltpu
from jax.sharding import Mesh, PartitionSpec as P

inverse_temp = 0.125
AXES = ("xh", "z", "y", "xl", "core")
SIZES = (2, 8, 8, 2, 2)
CHAN = ("xl", "core")
HALF = 64
ROWS = 512
KEYS = 1024
WIDE = 256
BLOCKS = KEYS // WIDE
PART = 32
f32, bf16 = jnp.float32, jnp.bfloat16


def device(xh, z, y, xl, core):
    return (((xh * 8 + z) * 8 + y) * 2 + xl) * 2 + core


MIXED = [
    [device(xh, z, y, xl, 0) for y in range(8) for xl in range(2)] for xh in range(2) for z in range(8)
] + [[device(xh, z, y, xl, 1) for xh in range(2) for z in range(8)] for y in range(8) for xl in range(2)]


WIDER = [
    [device(xh, z, y, xl, 0) for y in range(8) for xh in range(2) for xl in range(2)] for z in range(8)
] + [[device(xh, z, y, xl, 1) for z in range(8) for xh in range(2) for xl in range(2)] for y in range(8)]


def mixed_exchange(pieces, groups):
    return lax.all_to_all(pieces, AXES, split_axis=0, concat_axis=0, axis_index_groups=groups)


def position():
    xh, z, y, xl, core = (lax.axis_index(a) for a in AXES)
    first = core == 0
    return core, jnp.where(first, y, z), jnp.where(first, z, y), xh == xl


def share_kernel(mine, out, turned):
    core = lax.axis_index("core")
    for t in range(2):
        turned[:, t * 128 : (t + 1) * 128] = jnp.concatenate(
            [mine[c * 128 + t * 64 : c * 128 + (t + 1) * 64, :] for c in range(2)], axis=0
        ).T
    for k in range(4):
        half = jnp.where(core == 0, k // 2, k % 2)
        share = turned[pl.ds(pl.multiple_of(half * HALF, HALF), HALF), :]
        for n in range(8):
            out[4 * n + k] = share


def block(data, n, t, at=slice(None)):
    cut = slice(t * 128, (t + 1) * 128)
    return jnp.concatenate([data[2 * n, at, cut], data[2 * n + 1, at, cut]], axis=1)


def blocks(data, first, count, t, at=slice(None)):
    return jnp.concatenate([block(data, first + k, t, at) for k in range(count)], axis=0)


def mask_chunk(chunk, first, shift, wanted):
    at = pl.ds(pl.multiple_of(first, HALF), HALF)
    lane = lax.broadcasted_iota(jnp.int32, (HALF, WIDE), 1) - jnp.where(wanted, shift, -4096)
    same = lane == lax.broadcasted_iota(jnp.int32, (HALF, WIDE), 0)
    chunk[at, :] = jnp.where(same, -1e30, chunk[at, :])


def scaled_product(left, right):
    scores = lax.dot_general(left, right, (((1,), (1,)), ((), ())), preferred_element_type=f32)
    return scores * inverse_temp


def stats_kernel(own, other, out, *score):
    core, line, other_line, overlaps = position()
    chunks = [(t, b) for t in range(2) for b in range(BLOCKS)]
    across = [blocks(other, 0, 16, t) for t in range(2)]

    def fill(n):
        t, b = chunks[n]
        score[n][...] = scaled_product(across[t], blocks(own, 4 * b, 4, t))
        for e in range(2):
            mask_chunk(
                score[n],
                (2 * other_line + e) * HALF,
                line % 2 * 128 + e * HALF,
                jnp.logical_and(overlaps, line // 2 == b),
            )

    parts = []
    fill(0)
    for n in range(len(chunks)):
        if n + 1 < len(chunks):
            fill(n + 1)
        s = score[n][...]
        top = jnp.max(s, axis=0, keepdims=True)
        part = top + jnp.log(jnp.sum(jnp.exp(s - top), axis=0, keepdims=True))
        parts += [part[:, :128], part[:, 128:]]
    out[...] = jnp.broadcast_to(jnp.concatenate(parts, axis=0)[None], out.shape)


def grad_kernel(own, other, parts, out, score, lse, high, low, picked_rows, students):
    core, line, other_line, overlaps = position()
    at_core = pl.ds(pl.multiple_of(core * PART, PART), PART)
    @pl.when(core < 2)
    def _():
        for n in range(16):
            to = slice(n * PART, (n + 1) * PART)
            for half in range(2):
                for t in range(2):
                    cut, at = slice(t * 128, (t + 1) * 128), slice(half * 128, (half + 1) * 128)
                    picked_rows[t, to, at] = own[2 * n + half, at_core, cut]
                    students[t, n * HALF : (n + 1) * HALF, at] = other[2 * n + half, :, cut]
        for t in range(2):
            rows = picked_rows[t]
            for b in range(BLOCKS):
                score[t, b] = scaled_product(rows, students[t, b * WIDE : (b + 1) * WIDE, :])

    for side in range(2):
        every = parts[side]
        top = jnp.max(every, axis=0)
        lse[side] = top + jnp.log(jnp.sum(jnp.exp(every - top[None]), axis=0))
    lane = lax.broadcasted_iota(jnp.int32, (PART, WIDE), 1)
    item = lax.broadcasted_iota(jnp.int32, (PART, WIDE), 0)
    for e in range(2):
        shift = jnp.where(overlaps, other_line % 2 * 128 + e * HALF + core * PART, -4096)
        same = lane - shift == item
        at = pl.ds(pl.multiple_of((2 * line + e) * PART, PART), PART)
        for t in range(2):
            old = score[t, other_line // 2, at, :]
            score[t, other_line // 2, at, :] = jnp.where(same, -1e30, old)
    mine, others = lse[core], lse[1 - core]

    def of_part(k):
        picked = []
        for c in range(2):
            starts = [e * HALF + c * PART for e in range(2)]
            picked.append(
                jnp.concatenate(
                    [mine[k + d : k + d + 1, at : at + PART] for d in range(2) for at in starts], axis=1
                )
            )
        return jnp.where(core == 0, picked[0], picked[1])

    for q in range(4):
        at = slice(q * 128, (q + 1) * 128)
        row = [jnp.broadcast_to(of_part(t * 8 + 2 * q), (128, 128)).T for t in range(2)]
        for b in range(BLOCKS):
            for h in range(2):
                prob = []
                for t in range(2):
                    s = score[t, b, at, h * 128 : (h + 1) * 128]
                    k = t * 8 + b * 2 + h
                    prob.append(jnp.exp(s - row[t]) + jnp.exp(s - others[k : k + 1, :]))
                tile = prob[0] - prob[1]
                top_half = tile.astype(bf16)
                to = slice((2 * b + h) * 128, (2 * b + h + 1) * 128)
                high[at, to] = top_half
                low[at, to] = (tile - top_half.astype(f32)).astype(bf16)
    part = jnp.dot(high[...], students[0], preferred_element_type=f32)
    part = part + jnp.dot(low[...], students[0], preferred_element_type=f32)
    for n in range(16):
        for half in range(2):
            out[2 * n + half] = part[n * PART : (n + 1) * PART, half * 128 : (half + 1) * 128]


def sum_kernel(terms, out):
    first = lax.axis_index("core") == 0
    sums = []
    for k in range(4):
        total = terms[k]
        for n in range(1, 8):
            total = total + terms[4 * n + k]
        sums.append(total * inverse_temp)
    out[:PART] = sums[0] + jnp.where(first, sums[1], sums[2])
    out[PART:] = sums[3] + jnp.where(first, sums[2], sums[1])


def turn_kernel(whole, out, turned):
    parts = [whole[k * 64 + half * PART : k * 64 + (half + 1) * PART] for half in range(2) for k in range(2)]
    turned[...] = jnp.concatenate(parts, axis=0).T
    out[...] = turned[pl.ds(pl.multiple_of(lax.axis_index("core") * 64, 64), 64), :]


VMEM = pl.BlockSpec(memory_space=pltpu.VMEM)
PARAMS = pltpu.CompilerParams(vmem_limit_bytes=40 * 1024 * 1024)


def call(kernel, shape, dtype, *args, scratch=()):
    return pl.pallas_call(
        kernel,
        out_shape=jax.ShapeDtypeStruct(shape, dtype),
        in_specs=[VMEM] * len(args),
        out_specs=VMEM,
        scratch_shapes=list(scratch),
        compiler_params=PARAMS,
    )(*args)


def body(student, teacher):
    mine = jnp.concatenate([student.T, teacher.T], axis=0)
    chip = lax.all_gather(mine, "core", axis=0, tiled=True)
    share = call(share_kernel, (32, HALF, 256), bf16, chip, scratch=[pltpu.VMEM((128, 256), bf16)])
    own = mixed_exchange(share, WIDER)
    other = lax.ppermute(own, "core", [(0, 1), (1, 0)])

    tiles = [pltpu.VMEM((KEYS, WIDE), f32)] * (2 * BLOCKS)
    pieces = call(stats_kernel, (16, 16, 128), f32, own, other, scratch=tiles)
    parts = lax.all_gather(mixed_exchange(pieces, MIXED), "core", axis=0)

    wide = pltpu.VMEM((ROWS, KEYS), bf16)
    scratch = [pltpu.VMEM((2, BLOCKS, ROWS, WIDE), f32), pltpu.VMEM((2, 16, 128), f32), wide, wide]
    scratch += [pltpu.VMEM((2, ROWS, 256), bf16), pltpu.VMEM((2, KEYS, 256), bf16)]
    part = call(grad_kernel, (32, PART, 128), f32, own, other, parts, scratch=scratch)
    terms = mixed_exchange(part, WIDER)
    total = call(sum_kernel, (HALF, 128), f32, terms)
    whole = lax.all_gather(total, "core", axis=0, tiled=True)
    return call(turn_kernel, (64, 128), f32, whole, scratch=[pltpu.VMEM((128, 128), f32)]).T


def solution(mesh):
    split = Mesh(mesh.devices.reshape(SIZES), AXES)
    spec = P(("xh", "z", "y"), CHAN)
    return jax.shard_map(
        body, mesh=split, in_specs=(spec, spec), out_specs=spec, check_vma=False
    )
```

```python
import jax
import jax.numpy as jnp
from jax import lax
from jax.experimental import pallas as pl
from jax.experimental.pallas import tpu as pltpu
from jax.sharding import Mesh, PartitionSpec as P

inverse_temp = 0.125
AXES = ("xh", "z", "y", "xl", "core")
SIZES = (2, 8, 8, 2, 2)
CHAN = ("xl", "core")
HALF = 64
ROWS = 512
KEYS = 1024
WIDE = 256
BLOCKS = KEYS // WIDE
PART = 32
f32, bf16 = jnp.float32, jnp.bfloat16


def device(xh, z, y, xl, core):
    return (((xh * 8 + z) * 8 + y) * 2 + xl) * 2 + core


MIXED = [
    [device(xh, z, y, xl, 0) for y in range(8) for xl in range(2)] for xh in range(2) for z in range(8)
] + [[device(xh, z, y, xl, 1) for xh in range(2) for z in range(8)] for y in range(8) for xl in range(2)]


WIDER = [
    [device(xh, z, y, xl, 0) for y in range(8) for xh in range(2) for xl in range(2)] for z in range(8)
] + [[device(xh, z, y, xl, 1) for z in range(8) for xh in range(2) for xl in range(2)] for y in range(8)]


def mixed_exchange(pieces, groups):
    return lax.all_to_all(pieces, AXES, split_axis=0, concat_axis=0, axis_index_groups=groups)


def position():
    xh, z, y, xl, core = (lax.axis_index(a) for a in AXES)
    first = core == 0
    return core, jnp.where(first, y, z), jnp.where(first, z, y), xh == xl


def share_kernel(mine, out, turned):
    core = lax.axis_index("core")
    for t in range(2):
        turned[:, t * 128 : (t + 1) * 128] = jnp.concatenate(
            [mine[c * 128 + t * 64 : c * 128 + (t + 1) * 64, :] for c in range(2)], axis=0
        ).T
    for k in range(4):
        half = jnp.where(core == 0, k // 2, k % 2)
        share = turned[pl.ds(pl.multiple_of(half * HALF, HALF), HALF), :]
        for n in range(8):
            out[4 * n + k] = share


def block(data, n, t, at=slice(None)):
    cut = slice(t * 128, (t + 1) * 128)
    return jnp.concatenate([data[2 * n, at, cut], data[2 * n + 1, at, cut]], axis=1)


def blocks(data, first, count, t, at=slice(None)):
    return jnp.concatenate([block(data, first + k, t, at) for k in range(count)], axis=0)


def mask_chunk(chunk, first, shift, wanted):
    at = pl.ds(pl.multiple_of(first, HALF), HALF)
    lane = lax.broadcasted_iota(jnp.int32, (HALF, WIDE), 1) - jnp.where(wanted, shift, -4096)
    same = lane == lax.broadcasted_iota(jnp.int32, (HALF, WIDE), 0)
    chunk[at, :] = jnp.where(same, -1e30, chunk[at, :])


def scaled_product(left, right):
    scores = lax.dot_general(left, right, (((1,), (1,)), ((), ())), preferred_element_type=f32)
    return scores * inverse_temp


def stats_kernel(own, other, out, *score):
    core, line, other_line, overlaps = position()
    chunks = [(t, b) for t in range(2) for b in range(BLOCKS)]
    across = [blocks(other, 0, 16, t) for t in range(2)]

    def fill(n):
        t, b = chunks[n]
        score[n][...] = scaled_product(across[t], blocks(own, 4 * b, 4, t))
        for e in range(2):
            mask_chunk(
                score[n],
                (2 * other_line + e) * HALF,
                line % 2 * 128 + e * HALF,
                jnp.logical_and(overlaps, line // 2 == b),
            )

    parts = []
    fill(0)
    for n in range(len(chunks)):
        if n + 1 < len(chunks):
            fill(n + 1)
        s = score[n][...]
        top = jnp.max(s, axis=0, keepdims=True)
        part = top + jnp.log(jnp.sum(jnp.exp(s - top), axis=0, keepdims=True))
        parts += [part[:, :128], part[:, 128:]]
    out[...] = jnp.broadcast_to(jnp.concatenate(parts, axis=0)[None], out.shape)


def grad_kernel(own, other, parts, out, score, lse, high, low, picked_rows, students):
    core, line, other_line, overlaps = position()
    at_core = pl.ds(pl.multiple_of(core * PART, PART), PART)
    @pl.when(core < 2)
    def _():
        for n in range(16):
            to = slice(n * PART, (n + 1) * PART)
            for half in range(2):
                for t in range(2):
                    cut, at = slice(t * 128, (t + 1) * 128), slice(half * 128, (half + 1) * 128)
                    picked_rows[t, to, at] = own[2 * n + half, at_core, cut]
                    students[t, n * HALF : (n + 1) * HALF, at] = other[2 * n + half, :, cut]
        for t in range(2):
            rows = picked_rows[t]
            for b in range(BLOCKS):
                score[t, b] = scaled_product(rows, students[t, b * WIDE : (b + 1) * WIDE, :])

    for side in range(2):
        every = parts[side]
        top = jnp.max(every, axis=0)
        lse[side] = top + jnp.log(jnp.sum(jnp.exp(every - top[None]), axis=0))
    lane = lax.broadcasted_iota(jnp.int32, (PART, WIDE), 1)
    item = lax.broadcasted_iota(jnp.int32, (PART, WIDE), 0)
    for e in range(2):
        shift = jnp.where(overlaps, other_line % 2 * 128 + e * HALF + core * PART, -4096)
        same = lane - shift == item
        at = pl.ds(pl.multiple_of((2 * line + e) * PART, PART), PART)
        for t in range(2):
            old = score[t, other_line // 2, at, :]
            score[t, other_line // 2, at, :] = jnp.where(same, -1e30, old)
    mine, others = lse[core], lse[1 - core]

    def of_part(k):
        picked = []
        for c in range(2):
            starts = [e * HALF + c * PART for e in range(2)]
            picked.append(
                jnp.concatenate(
                    [mine[k + d : k + d + 1, at : at + PART] for d in range(2) for at in starts], axis=1
                )
            )
        return jnp.where(core == 0, picked[0], picked[1])

    for q in range(4):
        at = slice(q * 128, (q + 1) * 128)
        row = [jnp.broadcast_to(of_part(t * 8 + 2 * q), (128, 128)).T for t in range(2)]
        for b in range(BLOCKS):
            for h in range(2):
                by_own, by_other = [], []
                for t in range(2):
                    s = score[t, b, at, h * 128 : (h + 1) * 128]
                    k = t * 8 + b * 2 + h
                    by_own.append(jnp.exp(s - row[t]))
                    by_other.append(jnp.exp(s - others[k : k + 1, :]))
                one, two = by_own[0] - by_own[1], by_other[0] - by_other[1]
                rounded = one.astype(bf16).astype(f32) + two.astype(bf16).astype(f32)
                tile = 0.5 * (one + two + rounded)
                top_half = tile.astype(bf16)
                to = slice((2 * b + h) * 128, (2 * b + h + 1) * 128)
                high[at, to] = top_half
                low[at, to] = (tile - top_half.astype(f32)).astype(bf16)
    part = jnp.dot(high[...], students[0], preferred_element_type=f32)
    part = (part + jnp.dot(low[...], students[0], preferred_element_type=f32)).astype(bf16)
    for n in range(16):
        for half in range(2):
            out[2 * n + half] = part[n * PART : (n + 1) * PART, half * 128 : (half + 1) * 128]


def sum_kernel(terms, out):
    first = lax.axis_index("core") == 0
    sums = []
    for k in range(4):
        total = terms[k].astype(f32)
        for n in range(1, 8):
            total = total + terms[4 * n + k].astype(f32)
        sums.append(total * inverse_temp)
    out[:PART] = sums[0] + jnp.where(first, sums[1], sums[2])
    out[PART:] = sums[3] + jnp.where(first, sums[2], sums[1])


def turn_kernel(whole, out, turned):
    parts = [whole[k * 64 + half * PART : k * 64 + (half + 1) * PART] for half in range(2) for k in range(2)]
    turned[...] = jnp.concatenate(parts, axis=0).T
    out[...] = turned[pl.ds(pl.multiple_of(lax.axis_index("core") * 64, 64), 64), :]


VMEM = pl.BlockSpec(memory_space=pltpu.VMEM)
PARAMS = pltpu.CompilerParams(vmem_limit_bytes=40 * 1024 * 1024)


def call(kernel, shape, dtype, *args, scratch=()):
    return pl.pallas_call(
        kernel,
        out_shape=jax.ShapeDtypeStruct(shape, dtype),
        in_specs=[VMEM] * len(args),
        out_specs=VMEM,
        scratch_shapes=list(scratch),
        compiler_params=PARAMS,
    )(*args)


def body(student, teacher):
    mine = jnp.concatenate([student.T, teacher.T], axis=0)
    chip = lax.all_gather(mine, "core", axis=0, tiled=True)
    share = call(share_kernel, (32, HALF, 256), bf16, chip, scratch=[pltpu.VMEM((128, 256), bf16)])
    own = mixed_exchange(share, WIDER)
    other = lax.ppermute(own, "core", [(0, 1), (1, 0)])

    tiles = [pltpu.VMEM((KEYS, WIDE), f32)] * (2 * BLOCKS)
    pieces = call(stats_kernel, (16, 16, 128), f32, own, other, scratch=tiles)
    parts = lax.all_gather(mixed_exchange(pieces, MIXED), "core", axis=0)

    wide = pltpu.VMEM((ROWS, KEYS), bf16)
    scratch = [pltpu.VMEM((2, BLOCKS, ROWS, WIDE), f32), pltpu.VMEM((2, 16, 128), f32), wide, wide]
    scratch += [pltpu.VMEM((2, ROWS, 256), bf16), pltpu.VMEM((2, KEYS, 256), bf16)]
    part = call(grad_kernel, (32, PART, 128), bf16, own, other, parts, scratch=scratch)
    terms = mixed_exchange(part, WIDER)
    total = call(sum_kernel, (HALF, 128), f32, terms)
    whole = lax.all_gather(total, "core", axis=0, tiled=True)
    return call(turn_kernel, (64, 128), f32, whole, scratch=[pltpu.VMEM((128, 128), f32)]).T


def solution(mesh):
    split = Mesh(mesh.devices.reshape(SIZES), AXES)
    spec = P(("xh", "z", "y"), CHAN)
    return jax.shard_map(
        body, mesh=split, in_specs=(spec, spec), out_specs=spec, check_vma=False
    )
```

```python
import functools

import jax
import jax.numpy as jnp
from jax import lax
from jax.experimental import pallas as pl
from jax.experimental.pallas import tpu as pltpu
from jax.sharding import Mesh, PartitionSpec as P

inverse_temp = 0.125
AXES = ("xh", "z", "y", "xl", "core")
SIZES = (2, 8, 8, 2, 2)
CHAN = ("xl", "core")
HALF = 64
ROWS = 512
KEYS = 1024
WIDE = 256
BLOCKS = KEYS // WIDE
PART = 32
f32, bf16 = jnp.float32, jnp.bfloat16


def device(xh, z, y, xl, core):
    return (((xh * 8 + z) * 8 + y) * 2 + xl) * 2 + core


MIXED = [
    [device(xh, z, y, xl, 0) for y in range(8) for xl in range(2)] for xh in range(2) for z in range(8)
] + [[device(xh, z, y, xl, 1) for xh in range(2) for z in range(8)] for y in range(8) for xl in range(2)]


WIDER = [
    [device(xh, z, y, xl, 0) for y in range(8) for xh in range(2) for xl in range(2)] for z in range(8)
] + [[device(xh, z, y, xl, 1) for z in range(8) for xh in range(2) for xl in range(2)] for y in range(8)]


def mixed_exchange(pieces, groups):
    return lax.all_to_all(pieces, AXES, split_axis=0, concat_axis=0, axis_index_groups=groups)


def position():
    xh, z, y, xl, core = (lax.axis_index(a) for a in AXES)
    first = core == 0
    return core, jnp.where(first, y, z), jnp.where(first, z, y), xh == xl


def share_kernel(mine, out, turned):
    core = lax.axis_index("core")
    for t in range(2):
        turned[:, t * 128 : (t + 1) * 128] = jnp.concatenate(
            [mine[c * 128 + t * 64 : c * 128 + (t + 1) * 64, :] for c in range(2)], axis=0
        ).T
    for k in range(4):
        half = jnp.where(core == 0, k // 2, k % 2)
        share = turned[pl.ds(pl.multiple_of(half * HALF, HALF), HALF), :]
        for n in range(8):
            out[4 * n + k] = share


def block(data, n, t, at=slice(None)):
    cut = slice(t * 128, (t + 1) * 128)
    return jnp.concatenate([data[2 * n, at, cut], data[2 * n + 1, at, cut]], axis=1)


def blocks(data, first, count, t, at=slice(None)):
    return jnp.concatenate([block(data, first + k, t, at) for k in range(count)], axis=0)


def mask_chunk(chunk, first, shift, wanted):
    at = pl.ds(pl.multiple_of(first, HALF), HALF)
    lane = lax.broadcasted_iota(jnp.int32, (HALF, WIDE), 1) - jnp.where(wanted, shift, -4096)
    same = lane == lax.broadcasted_iota(jnp.int32, (HALF, WIDE), 0)
    chunk[at, :] = jnp.where(same, -1e30, chunk[at, :])


def scaled_product(left, right):
    scores = lax.dot_general(left, right, (((1,), (1,)), ((), ())), preferred_element_type=f32)
    return scores * inverse_temp


def stats_kernel(own, other, out, *score):
    core, line, other_line, overlaps = position()
    chunks = [(t, b) for t in range(2) for b in range(BLOCKS)]
    across = [blocks(other, 0, 16, t) for t in range(2)]

    def fill(n):
        t, b = chunks[n]
        score[n][...] = scaled_product(across[t], blocks(own, 4 * b, 4, t))
        for e in range(2):
            mask_chunk(
                score[n],
                (2 * other_line + e) * HALF,
                line % 2 * 128 + e * HALF,
                jnp.logical_and(overlaps, line // 2 == b),
            )

    def run(t):
        parts = []
        fill(4 * t)
        for n in range(4 * t, 4 * t + 4):
            if n < 4 * t + 3:
                fill(n + 1)
            s = score[n][...]
            top = jnp.max(s, axis=0, keepdims=True)
            part = top + jnp.log(jnp.sum(jnp.exp(s - top), axis=0, keepdims=True))
            parts += [part[:, :128], part[:, 128:]]
        lines = jnp.concatenate(parts, axis=0)
        out[:, t * 8 : (t + 1) * 8, :] = jnp.broadcast_to(lines[None], (16, 8, 128))

    for t in range(2):
        pl.when(core < 2)(functools.partial(run, t))


def grad_kernel(own, other, parts, out, score, lse, high, low, picked_rows, students):
    core, line, other_line, overlaps = position()
    at_core = pl.ds(pl.multiple_of(core * PART, PART), PART)
    @pl.when(core < 2)
    def _():
        for n in range(16):
            to = slice(n * PART, (n + 1) * PART)
            for half in range(2):
                for t in range(2):
                    cut, at = slice(t * 128, (t + 1) * 128), slice(half * 128, (half + 1) * 128)
                    picked_rows[t, to, at] = own[2 * n + half, at_core, cut]
                    students[t, n * HALF : (n + 1) * HALF, at] = other[2 * n + half, :, cut]
        for t in range(2):
            rows = picked_rows[t]
            for b in range(BLOCKS):
                score[t, b] = scaled_product(rows, students[t, b * WIDE : (b + 1) * WIDE, :])

    for side in range(2):
        every = parts[side]
        top = jnp.max(every, axis=0)
        lse[side] = top + jnp.log(jnp.sum(jnp.exp(every - top[None]), axis=0))
    lane = lax.broadcasted_iota(jnp.int32, (PART, WIDE), 1)
    item = lax.broadcasted_iota(jnp.int32, (PART, WIDE), 0)
    for e in range(2):
        shift = jnp.where(overlaps, other_line % 2 * 128 + e * HALF + core * PART, -4096)
        same = lane - shift == item
        at = pl.ds(pl.multiple_of((2 * line + e) * PART, PART), PART)
        for t in range(2):
            old = score[t, other_line // 2, at, :]
            score[t, other_line // 2, at, :] = jnp.where(same, -1e30, old)
    mine, others = lse[core], lse[1 - core]

    def of_part(k):
        picked = []
        for c in range(2):
            starts = [e * HALF + c * PART for e in range(2)]
            picked.append(
                jnp.concatenate(
                    [mine[k + d : k + d + 1, at : at + PART] for d in range(2) for at in starts], axis=1
                )
            )
        return jnp.where(core == 0, picked[0], picked[1])

    for q in range(4):
        at = slice(q * 128, (q + 1) * 128)
        row = [jnp.broadcast_to(of_part(t * 8 + 2 * q), (128, 128)).T for t in range(2)]
        for b in range(BLOCKS):
            for h in range(2):
                by_own, by_other = [], []
                for t in range(2):
                    s = score[t, b, at, h * 128 : (h + 1) * 128]
                    k = t * 8 + b * 2 + h
                    by_own.append(jnp.exp(s - row[t]))
                    by_other.append(jnp.exp(s - others[k : k + 1, :]))
                one, two = by_own[0] - by_own[1], by_other[0] - by_other[1]
                rounded = one.astype(bf16).astype(f32) + two.astype(bf16).astype(f32)
                tile = 0.5 * (one + two + rounded)
                top_half = tile.astype(bf16)
                to = slice((2 * b + h) * 128, (2 * b + h + 1) * 128)
                high[at, to] = top_half
                low[at, to] = (tile - top_half.astype(f32)).astype(bf16)
    part = jnp.dot(high[...], students[0], preferred_element_type=f32)
    part = (part + jnp.dot(low[...], students[0], preferred_element_type=f32)).astype(bf16)
    for n in range(16):
        for half in range(2):
            out[2 * n + half] = part[n * PART : (n + 1) * PART, half * 128 : (half + 1) * 128]


def sum_kernel(terms, out):
    first = lax.axis_index("core") == 0
    sums = []
    for k in range(4):
        total = terms[k].astype(f32)
        for n in range(1, 8):
            total = total + terms[4 * n + k].astype(f32)
        sums.append(total * inverse_temp)
    out[:PART] = sums[0] + jnp.where(first, sums[1], sums[2])
    out[PART:] = sums[3] + jnp.where(first, sums[2], sums[1])


def turn_kernel(whole, out, turned):
    parts = [whole[k * 64 + half * PART : k * 64 + (half + 1) * PART] for half in range(2) for k in range(2)]
    turned[...] = jnp.concatenate(parts, axis=0).T
    out[...] = turned[pl.ds(pl.multiple_of(lax.axis_index("core") * 64, 64), 64), :]


VMEM = pl.BlockSpec(memory_space=pltpu.VMEM)
PARAMS = pltpu.CompilerParams(vmem_limit_bytes=40 * 1024 * 1024)


def call(kernel, shape, dtype, *args, scratch=()):
    return pl.pallas_call(
        kernel,
        out_shape=jax.ShapeDtypeStruct(shape, dtype),
        in_specs=[VMEM] * len(args),
        out_specs=VMEM,
        scratch_shapes=list(scratch),
        compiler_params=PARAMS,
    )(*args)


def body(student, teacher):
    mine = jnp.concatenate([student.T, teacher.T], axis=0)
    chip = lax.all_gather(mine, "core", axis=0, tiled=True)
    share = call(share_kernel, (32, HALF, 256), bf16, chip, scratch=[pltpu.VMEM((128, 256), bf16)])
    own = mixed_exchange(share, WIDER)
    other = lax.ppermute(own, "core", [(0, 1), (1, 0)])

    tiles = [pltpu.VMEM((KEYS, WIDE), f32)] * (2 * BLOCKS)
    pieces = call(stats_kernel, (16, 16, 128), f32, own, other, scratch=tiles)
    parts = lax.all_gather(mixed_exchange(pieces, MIXED), "core", axis=0)

    wide = pltpu.VMEM((ROWS, KEYS), bf16)
    scratch = [pltpu.VMEM((2, BLOCKS, ROWS, WIDE), f32), pltpu.VMEM((2, 16, 128), f32), wide, wide]
    scratch += [pltpu.VMEM((2, ROWS, 256), bf16), pltpu.VMEM((2, KEYS, 256), bf16)]
    part = call(grad_kernel, (32, PART, 128), bf16, own, other, parts, scratch=scratch)
    terms = mixed_exchange(part, WIDER)
    total = call(sum_kernel, (HALF, 128), f32, terms)
    whole = lax.all_gather(total, "core", axis=0, tiled=True)
    return call(turn_kernel, (64, 128), f32, whole, scratch=[pltpu.VMEM((128, 128), f32)]).T


def solution(mesh):
    split = Mesh(mesh.devices.reshape(SIZES), AXES)
    spec = P(("xh", "z", "y"), CHAN)
    return jax.shard_map(
        body, mesh=split, in_specs=(spec, spec), out_specs=spec, check_vma=False
    )
```
